512 devices in a mesh: src: 16 (over z), tgt: 32 (over y, x, core).
Axes of the slice: x: 4, y: 4, z: 16, core: 2. Of those that a mesh axis runs over, the one named last changes fastest.
Arguments:
- source_emb: bfloat16 [16384, 1024], P('src', 'tgt'), may hold values from -1100 to 1100
- target_emb: bfloat16 [32768, 1024], P('tgt', 'src'), may hold values from -1100 to 1100
- src_group: int32 [16384], P('src'), may hold values from 0 to 7, as said below
- tgt_group: int32 [32768], P('tgt'), may hold values from 0 to 7, as said below
Outputs:
- margins: float32 [16384, 32768], P('src', 'tgt')
The draws below stay inside these ranges and needn't reach their ends.
Inputs may be any that keep to these rules, and one draw needn't show every extreme that they name: `src_group`: every block from 0 to 7 labels at least one source sentence. `tgt_group`: every block from 0 to 7 labels at least two target sentences.
All inputs are finite; a program needn't handle non-finite values.
Results may differ from the reference program's by a relative error of at most 0.0003.
Values may be sent and summed in bfloat16 or wider, within the bound.
No kernel may reach another device: no remote copies, remote signals or barrier semaphores. Data moves between devices by JAX's collectives and lax.ppermute only.
A program may use at most 64 MiB of HBM per device.

```python
import math
import jax
import jax.numpy as jnp
from jax import lax

D = 1024
SRC_DEV = 1024
GROUPS = 8
NS = 16384
NT = 32768


def group_labels(key):
    keys = jax.random.split(jax.random.fold_in(key, 101), 5)
    relabel = jax.random.permutation(keys[0], GROUPS).astype(jnp.int32)
    src_raw = jnp.min(jax.random.randint(keys[1], (3, NS), 0, GROUPS), axis=0)
    tgt_raw = jnp.min(jax.random.randint(keys[2], (3, NT), 0, GROUPS), axis=0)
    src_labels = relabel[src_raw]
    tgt_labels = relabel[tgt_raw]
    every = jnp.arange(GROUPS, dtype=jnp.int32)
    src_places = jax.random.permutation(keys[3], NS)[:GROUPS]
    src_labels = src_labels.at[src_places].set(every)
    tgt_places = jax.random.permutation(keys[4], NT)[:2 * GROUPS]
    tgt_labels = tgt_labels.at[tgt_places].set(jnp.concatenate([every, every]))
    return (src_labels.astype(jnp.int32), tgt_labels.astype(jnp.int32))


def scaled(core, key, count, highest):
    keys = jax.random.split(key, 2)
    feature = jnp.exp(jax.random.uniform(keys[0], (1, D), jnp.float32, 0.0, math.log(highest)))
    rowwise = jnp.exp(jax.random.uniform(keys[1], (count, 1), jnp.float32, 0.0, math.log(highest)))
    return core * feature * rowwise


def draw_source_emb(key, part):
    key = jax.random.fold_in(key, 1)
    keys = jax.random.split(key, 3)
    core = jnp.clip(jax.random.normal(keys[0], (NS, D), jnp.float32), -5.0, 5.0)
    values = scaled(core, keys[2], NS, 10.0)
    return values.astype(jnp.bfloat16)


def draw_target_emb(key, part):
    key = jax.random.fold_in(key, 2)
    keys = jax.random.split(key, 3)
    core = jnp.clip(jax.random.normal(keys[0], (NT, D), jnp.float32), -5.0, 5.0)
    values = scaled(core, keys[2], NT, 10.0)
    return values.astype(jnp.bfloat16)


def draw_src_group(key, part):
    src_labels, tgt_labels = group_labels(key)
    return src_labels


def draw_tgt_group(key, part):
    src_labels, tgt_labels = group_labels(key)
    return tgt_labels


def setup_inputs(seed: int = 0) -> dict:
    splits = jax.random.split(jax.random.key(seed), 5)
    source_emb = draw_source_emb(jax.random.fold_in(splits[4], 71), 0)
    target_emb = draw_target_emb(jax.random.fold_in(splits[4], 71), 0)
    src_group = draw_src_group(jax.random.fold_in(splits[4], 71), 0)
    tgt_group = draw_tgt_group(jax.random.fold_in(splits[4], 71), 0)
    return dict(source_emb=source_emb, target_emb=target_emb, src_group=src_group, tgt_group=tgt_group)


smoothing_divisor = 256.0
floor_value = -1e+30
eps = 1e-06

def inverse_norm(sentences):
    widened_values = sentences.astype(jnp.float32)
    return lax.rsqrt(lax.optimization_barrier(jnp.sum(widened_values * widened_values, axis=1)) + eps)

def pair_level(row_level, col_level):
    highest = jnp.maximum(row_level, col_level)
    return highest + jnp.log1p(jnp.exp(-jnp.abs(row_level - col_level)))

def reference(source_emb, target_emb, src_group, tgt_group):
    left_neighbor_norm = inverse_norm(source_emb)
    right_neighbor_norm = inverse_norm(target_emb)
    blocks = NS // SRC_DEV
    src_rows = source_emb.reshape(blocks, SRC_DEV, D)
    src_scales = left_neighbor_norm.reshape(blocks, SRC_DEV)
    src_labels = src_group.reshape(blocks, SRC_DEV)

    def sweep_rows(totals, element):
        col_max, col_sum = totals
        sentences, ratio_gap_factor, labels = element
        cosine_inner_matrix = lax.dot_general(sentences, target_emb, (((1,), (1,)), ((), ())), preferred_element_type=jnp.float32)
        bitext_rating_matrix = smoothing_divisor * cosine_inner_matrix * ratio_gap_factor[:, None] * right_neighbor_norm[None, :]
        allowed = labels[:, None] == tgt_group[None, :]
        weight = allowed.astype(jnp.float32)
        masked_scores = jnp.where(allowed, bitext_rating_matrix, floor_value)
        row_max = lax.optimization_barrier(jnp.max(masked_scores, axis=1))
        row_sum = lax.optimization_barrier(jnp.sum(weight * jnp.exp(masked_scores - row_max[:, None]), axis=1))
        row_level = row_max + jnp.log(row_sum)
        block_max = lax.optimization_barrier(jnp.max(masked_scores, axis=0))
        new_max = jnp.maximum(col_max, block_max)
        col_sum = col_sum * jnp.exp(col_max - new_max) + lax.optimization_barrier(jnp.sum(weight * jnp.exp(masked_scores - new_max[None, :]), axis=0))
        return ((new_max, col_sum), (bitext_rating_matrix, row_level))
    initial = (jnp.full((NT,), floor_value, jnp.float32), jnp.zeros((NT,), jnp.float32))
    (col_max, col_sum), (all_scores, row_levels) = lax.scan(sweep_rows, initial, (src_rows, src_scales, src_labels))
    col_level = col_max + jnp.log(col_sum)

    def finish(element):
        bitext_rating_matrix, row_level, labels = element
        allowed = labels[:, None] == tgt_group[None, :]
        margin = bitext_rating_matrix - pair_level(row_level[:, None], col_level[None, :]) + math.log(2.0)
        return jnp.where(allowed, margin, jnp.zeros_like(margin))
    margins = lax.map(finish, (all_scores, row_levels, src_labels))
    return margins.reshape(NS, NT)
```

```python
import math

import jax
import jax.numpy as jnp
from jax import lax
from jax.experimental import pallas as pl
from jax.experimental.pallas import tpu as pltpu
from jax.sharding import PartitionSpec as P

smoothing_divisor = 256.0
floor_value = -1e30
absent_below = -1e29
eps = 1e-06
lanes = 128


def log_sum_exp(levels):
    highest = jnp.max(levels, axis=0)
    return highest + jnp.log(jnp.sum(jnp.exp(levels - highest[None]), axis=0))


def as_column(line):
    return jnp.transpose(jnp.broadcast_to(line, (lanes, lanes)))


def as_line(column):
    return jnp.transpose(jnp.broadcast_to(column, (lanes, lanes)))[:1]


def score_kernel(pieces, place, *refs):
    source, source_group, target_group = refs[:3]
    piece_refs = refs[3 : 3 + len(pieces)]
    scores, row_out, col_out = refs[3 + len(pieces) : 6 + len(pieces)]
    gathered, scale_cols, group_cols = refs[6 + len(pieces) :]
    z = place[0]
    chunks, depth, columns = gathered.shape
    rows = source.shape[0]
    squares = jnp.zeros((8, columns), jnp.float32)
    for offsets, ref in zip(pieces, piece_refs):
        for k, offset in enumerate(offsets):
            block = ref[k]
            gathered[lax.rem(z + (offset + chunks), chunks)] = block
            wide = block.astype(jnp.float32)
            squares += jnp.sum((wide * wide).reshape(depth // 8, 8, columns), axis=0)
    target_scale = lax.rsqrt(jnp.sum(squares, axis=0, keepdims=True) + eps)

    wide_rows = rows // lanes
    for i in range(wide_rows):
        part = source[pl.ds(i * lanes, lanes), :].astype(jnp.float32)
        norm = lax.rsqrt(jnp.sum(part * part, axis=1, keepdims=True) + eps)
        scale_cols[pl.ds(i * lanes, lanes), :] = jnp.broadcast_to(
            smoothing_divisor * norm, (lanes, lanes)
        )
        group_cols[pl.ds(i * lanes, lanes), :] = as_column(source_group[i : i + 1, :])

    width = 256
    flat = gathered.reshape(chunks * depth, columns)
    target_groups = jnp.concatenate([target_group[i : i + 1, :] for i in range(columns // lanes)], axis=1)
    for n in range(columns // width):
        span = slice(n * width, (n + 1) * width)
        products = jnp.dot(source[...], flat[:, span], preferred_element_type=jnp.float32)
        scaled = products * scale_cols[:, :1] * target_scale[:, span]
        allowed = group_cols[:, :1] == target_groups[:, span]
        scores[:, span] = jnp.where(allowed, scaled, floor_value)

    col_max = jnp.max(scores[...], axis=0, keepdims=True)
    col_sum = jnp.zeros((1, columns), jnp.float32)
    row_lines = []
    for i in range(wide_rows):
        part = scores[pl.ds(i * lanes, lanes), :]
        row_max = jnp.max(part, axis=1, keepdims=True)
        row_sum = jnp.sum(jnp.exp(part - row_max), axis=1, keepdims=True)
        level = jnp.where(row_max < absent_below, floor_value, row_max + jnp.log(row_sum))
        row_lines.append(as_line(level))
        col_sum += jnp.sum(jnp.exp(part - col_max), axis=0, keepdims=True)
    row_out[...] = jnp.concatenate(row_lines, axis=0)
    col_level = jnp.where(col_max < absent_below, floor_value, col_max + jnp.log(col_sum))
    col_out[...] = jnp.concatenate(
        [col_level[:, i * lanes : (i + 1) * lanes] for i in range(columns // lanes)], axis=0
    )


def margin_kernel(scores, row_levels, col_levels, margins, row_column, col_line):
    i = pl.program_id(0)

    @pl.when(i == 0)
    def _():
        rows = log_sum_exp(row_levels[...])
        for k in range(rows.shape[0]):
            row_column[k] = as_column(rows[k : k + 1, :])
        cols = log_sum_exp(col_levels[...])
        col_line[...] = jnp.concatenate([cols[k : k + 1, :] for k in range(cols.shape[0])], axis=1)

    part = scores[...]
    row = row_column[i][:, :1]
    col = col_line[...]
    pair = jnp.maximum(row, col) + jnp.log(1.0 + jnp.exp(-jnp.abs(row - col)))
    margins[...] = jnp.where(part < absent_below, 0.0, part - pair + math.log(2.0))


def local(source_emb, target_emb, src_group, tgt_group):
    z_size = lax.axis_size("src")
    t_size = lax.axis_size("tgt")

    def shift(x, step):
        return lax.ppermute(x, "src", [(i, (i + step) % z_size) for i in range(z_size)])

    own = target_emb.T
    low, high = shift(own, 5), shift(own, -5)
    three = jnp.stack([own, low, high])
    one, mone = shift(three, 1), shift(three, -1)
    two, mtwo = shift(three, 2), shift(three, -2)
    far = shift(low, 3)
    pieces = [
        ((0, -5, 5), three),
        ((-1, -6, 4), one),
        ((1, -4, 6), mone),
        ((-2, -7, 3), two),
        ((2, -3, 7), mtwo),
        ((-8,), far[None]),
    ]
    part = source_emb.T
    sources = lax.all_to_all(jnp.broadcast_to(part[None], (t_size,) + part.shape), "tgt", 0, 0)
    sources = sources.reshape(-1, sources.shape[-1]).T

    rows, columns, chunks = sources.shape[0], own.shape[1], z_size
    place = lax.axis_index("src").astype(jnp.int32).reshape(1)
    vmem = pl.BlockSpec(memory_space=pltpu.VMEM)
    scores, row_level, col_level = pl.pallas_call(
        lambda *refs: score_kernel([p for p, _ in pieces], *refs),
        out_shape=(
            jax.ShapeDtypeStruct((rows, columns), jnp.float32),
            jax.ShapeDtypeStruct((rows // lanes, lanes), jnp.float32),
            jax.ShapeDtypeStruct((columns // lanes, lanes), jnp.float32),
        ),
        in_specs=[pl.BlockSpec(memory_space=pltpu.SMEM)] + [vmem] * (3 + len(pieces)),
        out_specs=(vmem, vmem, vmem),
        scratch_shapes=[
            pltpu.VMEM((chunks, own.shape[0], columns), jnp.bfloat16),
            pltpu.VMEM((rows, lanes), jnp.float32),
            pltpu.VMEM((rows, lanes), jnp.int32),
        ],
        compiler_params=pltpu.CompilerParams(vmem_limit_bytes=48 * 2**20),
        name="scores",
    )(place, sources, src_group.reshape(-1, lanes), tgt_group.reshape(-1, lanes), *[x for _, x in pieces])

    col_levels = lax.all_to_all(jnp.broadcast_to(col_level[None], (z_size,) + col_level.shape), "src", 0, 0)
    row_levels = lax.all_to_all(jnp.broadcast_to(row_level[None], (t_size,) + row_level.shape), "tgt", 0, 0)

    return pl.pallas_call(
        margin_kernel,
        grid=(rows // lanes,),
        out_shape=jax.ShapeDtypeStruct((rows, columns), jnp.float32),
        in_specs=[
            pl.BlockSpec((lanes, columns), lambda i: (i, 0)),
            pl.BlockSpec(row_levels.shape, lambda i: (0, 0, 0)),
            pl.BlockSpec(col_levels.shape, lambda i: (0, 0, 0)),
        ],
        out_specs=pl.BlockSpec((lanes, columns), lambda i: (i, 0)),
        scratch_shapes=[
            pltpu.VMEM((rows // lanes, lanes, lanes), jnp.float32),
            pltpu.VMEM((1, columns), jnp.float32),
        ],
        compiler_params=pltpu.CompilerParams(vmem_limit_bytes=32 * 2**20),
        name="margins",
    )(scores, row_levels, col_levels)


def solution(mesh):
    in_specs = (P("src", "tgt"), P("tgt", "src"), P("src"), P("tgt"))
    out_specs = P("src", "tgt")
    return jax.shard_map(local, mesh=mesh, in_specs=in_specs, out_specs=out_specs, check_vma=False)
```

```python
import math

import jax
import jax.numpy as jnp
from jax import lax
from jax.experimental import pallas as pl
from jax.experimental.pallas import tpu as pltpu
from jax.sharding import PartitionSpec as P

smoothing_divisor = 256.0
floor_value = -1e30
absent_below = -1e29
eps = 1e-06
lanes = 128
code_scale = 512.0


def encode(x):
    wide = x.astype(jnp.float32)
    root = jnp.sqrt(jnp.abs(wide)) * code_scale
    return jnp.where(wide < 0, -root, root).astype(jnp.float16)


def decode(code):
    wide = code.astype(jnp.float32)
    return (wide * jnp.abs(wide) * (1.0 / code_scale**2)).astype(jnp.bfloat16)


def log_sum_exp(levels):
    highest = jnp.max(levels, axis=0)
    return highest + jnp.log(jnp.sum(jnp.exp(levels - highest[None]), axis=0))


def as_column(line):
    return jnp.transpose(jnp.broadcast_to(line, (lanes, lanes)))


def as_line(column):
    return jnp.transpose(jnp.broadcast_to(column, (lanes, lanes)))[:1]


def inverse_norm(features):
    depth, count = features.shape
    squares = jnp.zeros((8, count), jnp.float32)
    step = 64
    for k in range(0, depth, step):
        wide = features[k : k + step, :].astype(jnp.float32)
        squares += jnp.sum((wide * wide).reshape(step // 8, 8, count), axis=0)
    return lax.rsqrt(jnp.sum(squares, axis=0, keepdims=True) + eps)


def score_kernel(source, target, source_group, target_group, scores, row_out, col_out, turned, scale_cols, group_cols):
    depth, rows = source.shape
    columns = target.shape[1]
    target_scale = inverse_norm(target)
    source_scale = inverse_norm(source) * smoothing_divisor
    for i in range(rows // lanes):
        block = slice(i * lanes, (i + 1) * lanes)
        scale_cols[block, :] = as_column(source_scale[:, block])
        group_cols[block, :] = as_column(source_group[i : i + 1, :])
        turned[block, :] = jnp.transpose(source[:, block])

    width = 256
    target_groups = jnp.concatenate([target_group[i : i + 1, :] for i in range(columns // lanes)], axis=1)
    for n in range(columns // width):
        span = slice(n * width, (n + 1) * width)
        products = jnp.dot(turned[...], target[:, span], preferred_element_type=jnp.float32)
        scaled = products * scale_cols[:, :1] * target_scale[:, span]
        allowed = group_cols[:, :1] == target_groups[:, span]
        scores[:, span] = jnp.where(allowed, scaled, floor_value)

    col_max = jnp.max(scores[...], axis=0, keepdims=True)
    col_sum = jnp.zeros((1, columns), jnp.float32)
    row_lines = []
    for i in range(rows // lanes):
        part = scores[i * lanes : (i + 1) * lanes, :]
        row_max = jnp.max(part, axis=1, keepdims=True)
        row_sum = jnp.sum(jnp.exp(part - row_max), axis=1, keepdims=True)
        level = jnp.where(row_max < absent_below, floor_value, row_max + jnp.log(row_sum))
        row_lines.append(as_line(level))
        col_sum += jnp.sum(jnp.exp(part - col_max), axis=0, keepdims=True)
    row_out[...] = jnp.concatenate(row_lines, axis=0)
    col_level = jnp.where(col_max < absent_below, floor_value, col_max + jnp.log(col_sum))
    col_out[...] = jnp.concatenate(
        [col_level[:, i * lanes : (i + 1) * lanes] for i in range(columns // lanes)], axis=0
    )


def margin_kernel(scores, row_levels, col_levels, margins, row_column, col_line):
    i = pl.program_id(0)

    @pl.when(i == 0)
    def _():
        rows = log_sum_exp(row_levels[...])
        for k in range(rows.shape[0]):
            row_column[k] = as_column(rows[k : k + 1, :])
        cols = log_sum_exp(col_levels[...])
        col_line[...] = jnp.concatenate([cols[k : k + 1, :] for k in range(cols.shape[0])], axis=1)

    part = scores[pl.ds(pl.multiple_of(i * lanes, lanes), lanes), :]
    row = row_column[i][:, :1]
    col = col_line[...]
    pair = jnp.maximum(row, col) + jnp.log(1.0 + jnp.exp(-jnp.abs(row - col)))
    margins[...] = jnp.where(part < absent_below, 0.0, part - pair + math.log(2.0))


def find_scores(source, target, src_group, tgt_group):
    rows, columns = source.shape[1], target.shape[1]
    vmem = pl.BlockSpec(memory_space=pltpu.VMEM)
    return pl.pallas_call(
        score_kernel,
        out_shape=(
            jax.ShapeDtypeStruct((rows, columns), jnp.float32),
            jax.ShapeDtypeStruct((rows // lanes, lanes), jnp.float32),
            jax.ShapeDtypeStruct((columns // lanes, lanes), jnp.float32),
        ),
        in_specs=[vmem] * 4,
        out_specs=(vmem, vmem, vmem),
        scratch_shapes=[
            pltpu.VMEM((rows, source.shape[0]), jnp.bfloat16),
            pltpu.VMEM((rows, lanes), jnp.float32),
            pltpu.VMEM((rows, lanes), jnp.int32),
        ],
        compiler_params=pltpu.CompilerParams(vmem_limit_bytes=48 * 2**20),
        name="scores",
    )(source, target, src_group.reshape(-1, lanes), tgt_group.reshape(-1, lanes))


def find_margins(scores, row_levels, col_levels):
    rows, columns = scores.shape
    vmem = pl.BlockSpec(memory_space=pltpu.VMEM)
    return pl.pallas_call(
        margin_kernel,
        grid=(rows // lanes,),
        out_shape=jax.ShapeDtypeStruct((rows, columns), jnp.float32),
        in_specs=[vmem, vmem, vmem],
        out_specs=pl.BlockSpec((lanes, columns), lambda i: (i, 0)),
        scratch_shapes=[
            pltpu.VMEM((rows // lanes, lanes, lanes), jnp.float32),
            pltpu.VMEM((1, columns), jnp.float32),
        ],
        compiler_params=pltpu.CompilerParams(vmem_limit_bytes=32 * 2**20),
        name="margins",
    )(scores, row_levels, col_levels)


def local(source_emb, target_emb, src_group, tgt_group):
    z_size = lax.axis_size("src")
    t_size = lax.axis_size("tgt")
    part = source_emb.T
    source = lax.all_to_all(jnp.broadcast_to(part[None], (t_size,) + part.shape), "tgt", 0, 0)
    source = source.reshape(-1, source.shape[-1])
    target = decode(lax.all_gather(encode(target_emb.T), "src", axis=0, tiled=True))
    scores, row_level, col_level = find_scores(source, target, src_group, tgt_group)
    col_levels = lax.all_to_all(jnp.broadcast_to(col_level[None], (z_size,) + col_level.shape), "src", 0, 0)
    row_levels = lax.all_to_all(jnp.broadcast_to(row_level[None], (t_size,) + row_level.shape), "tgt", 0, 0)
    return find_margins(scores, row_levels, col_levels)


def solution(mesh):
    in_specs = (P("src", "tgt"), P("tgt", "src"), P("src"), P("tgt"))
    out_specs = P("src", "tgt")
    return jax.shard_map(local, mesh=mesh, in_specs=in_specs, out_specs=out_specs, check_vma=False)
```

```python
import math

import jax
import jax.numpy as jnp
from jax import lax
from jax.experimental import pallas as pl
from jax.experimental.pallas import tpu as pltpu
from jax.sharding import PartitionSpec as P

smoothing_divisor = 256.0
floor_value = -1e30
absent_below = -1e29
eps = 1e-06
lanes = 128
code_scale = 512.0
log2_e = math.log2(math.e)


def encode(x):
    wide = x.astype(jnp.float32)
    root = jnp.sqrt(jnp.abs(wide)) * code_scale
    return jnp.where(wide < 0, -root, root).astype(jnp.float16)


def decode(code):
    wide = code.astype(jnp.float32)
    return (wide * jnp.abs(wide) * (1.0 / code_scale**2)).astype(jnp.bfloat16)


def log_sum(levels):
    highest = jnp.max(levels, axis=0)
    return highest + jnp.log2(jnp.sum(jnp.exp2(levels - highest[None]), axis=0))


def as_column(line):
    return jnp.transpose(jnp.broadcast_to(line, (lanes, lanes)))


def as_line(column):
    return jnp.transpose(jnp.broadcast_to(column, (lanes, lanes)))[:1]


def joined(lines):
    return jnp.concatenate([lines[i : i + 1, :] for i in range(lines.shape[0])], axis=1)


def level(highest, total):
    return jnp.where(highest < absent_below, floor_value, highest + jnp.log2(total))


def inverse_norm(features):
    depth, count = features.shape
    squares = jnp.zeros((8, count), jnp.float32)
    step = 64
    for k in range(0, depth, step):
        wide = features[k : k + step, :].astype(jnp.float32)
        squares += jnp.sum((wide * wide).reshape(step // 8, 8, count), axis=0)
    return lax.rsqrt(jnp.sum(squares, axis=0, keepdims=True) + eps)


def score_kernel(
    source_far, target, source_group, target_group, scores, row_out, col_out, source, turned, scale_cols, group_cols, sems
):
    depth, rows = source.shape
    columns = target.shape[1]
    size = depth // sems.shape[0]
    fetches = []
    for k in range(sems.shape[0]):
        block = slice(k * size, (k + 1) * size)
        fetches.append(pltpu.make_async_copy(source_far.at[block, :], source.at[block, :], sems.at[k]))
        fetches[-1].start()
    target_scale = inverse_norm(target)
    for i in range(rows // lanes):
        group_cols[i * lanes : (i + 1) * lanes, :] = as_column(source_group[i : i + 1, :])
    for k, fetch in enumerate(fetches):
        fetch.wait()
        block = slice(k * size, (k + 1) * size)
        for i in range(rows // lanes):
            span = slice(i * lanes, (i + 1) * lanes)
            turned[span, block] = jnp.transpose(source[block, span])
    source_scale = inverse_norm(source) * (smoothing_divisor * log2_e)
    for i in range(rows // lanes):
        span = slice(i * lanes, (i + 1) * lanes)
        scale_cols[span, :] = as_column(source_scale[:, span])

    products = jnp.dot(turned[...], target[...], preferred_element_type=jnp.float32)
    scaled = products * scale_cols[:, :1] * target_scale
    allowed = group_cols[:, :1] == joined(target_group)
    scores[...] = jnp.where(allowed, scaled, floor_value)

    col_max = jnp.max(scores[...], axis=0, keepdims=True)
    col_sum = jnp.zeros((1, columns), jnp.float32)
    row_lines = []
    for i in range(rows // lanes):
        part = scores[i * lanes : (i + 1) * lanes, :]
        row_max = jnp.max(part, axis=1, keepdims=True)
        row_sum = jnp.sum(jnp.exp2(part - row_max), axis=1, keepdims=True)
        row_lines.append(as_line(level(row_max, row_sum)))
        col_sum += jnp.sum(jnp.exp2(part - col_max), axis=0, keepdims=True)
    row_out[...] = jnp.concatenate(row_lines, axis=0)
    col_level = level(col_max, col_sum)
    col_out[...] = jnp.concatenate(
        [col_level[:, i * lanes : (i + 1) * lanes] for i in range(columns // lanes)], axis=0
    )


def margin_kernel(scores, row_levels, col_levels, margins, ready, sems):
    rows = log_sum(row_levels[...]) - 1.0
    col = joined(log_sum(col_levels[...]) - 1.0)
    copies = []
    for i in range(rows.shape[0]):
        block = slice(i * lanes, (i + 1) * lanes)
        part = scores[block, :]
        row = as_column(rows[i : i + 1, :])[:, :1]
        pair = jnp.maximum(row, col) + jnp.log2(1.0 + jnp.exp2(-jnp.abs(row - col)))
        ready[block, :] = jnp.where(part < absent_below, 0.0, (part - pair) * (1.0 / log2_e))
        copies.append(pltpu.make_async_copy(ready.at[block, :], margins.at[block, :], sems.at[i]))
        copies[-1].start()
    for copy in copies:
        copy.wait()


def spread_kernel(part, copies, sem):
    for k in range(copies.shape[0]):
        pltpu.make_async_copy(part, copies.at[k], sem).start()
    for k in range(copies.shape[0]):
        pltpu.make_async_copy(part, copies.at[k], sem).wait()


def spread(part, count):
    return pl.pallas_call(
        spread_kernel,
        out_shape=jax.ShapeDtypeStruct((count,) + part.shape, part.dtype),
        in_specs=[pl.BlockSpec(memory_space=pltpu.VMEM)],
        out_specs=pl.BlockSpec(memory_space=pltpu.HBM),
        scratch_shapes=[pltpu.SemaphoreType.DMA],
        name="spread",
    )(part)


def find_scores(source, target, src_group, tgt_group):
    rows, columns = source.shape[1], target.shape[1]
    vmem = pl.BlockSpec(memory_space=pltpu.VMEM)
    return pl.pallas_call(
        score_kernel,
        out_shape=(
            jax.ShapeDtypeStruct((rows, columns), jnp.float32),
            jax.ShapeDtypeStruct((rows // lanes, lanes), jnp.float32),
            jax.ShapeDtypeStruct((columns // lanes, lanes), jnp.float32),
        ),
        in_specs=[pl.BlockSpec(memory_space=pltpu.HBM), vmem, vmem, vmem],
        out_specs=(vmem, vmem, vmem),
        scratch_shapes=[
            pltpu.VMEM(source.shape, jnp.bfloat16),
            pltpu.VMEM((rows, source.shape[0]), jnp.bfloat16),
            pltpu.VMEM((rows, lanes), jnp.float32),
            pltpu.VMEM((rows, lanes), jnp.int32),
            pltpu.SemaphoreType.DMA((4,)),
        ],
        compiler_params=pltpu.CompilerParams(vmem_limit_bytes=20 * 2**20),
        name="scores",
    )(source, target, src_group.reshape(-1, lanes), tgt_group.reshape(-1, lanes))


def find_margins(scores, row_levels, col_levels):
    rows, columns = scores.shape
    vmem = pl.BlockSpec(memory_space=pltpu.VMEM)
    return pl.pallas_call(
        margin_kernel,
        out_shape=jax.ShapeDtypeStruct((rows, columns), jnp.float32),
        in_specs=[vmem, vmem, vmem],
        out_specs=pl.BlockSpec(memory_space=pl.ANY),
        scratch_shapes=[
            pltpu.VMEM((rows, columns), jnp.float32),
            pltpu.SemaphoreType.DMA((rows // lanes,)),
        ],
        compiler_params=pltpu.CompilerParams(vmem_limit_bytes=16 * 2**20),
        name="margins",
    )(scores, row_levels, col_levels)


def local(source_emb, target_emb, src_group, tgt_group):
    z_size = lax.axis_size("src")
    t_size = lax.axis_size("tgt")
    source = lax.all_to_all(spread(source_emb.T, t_size), "tgt", 0, 0)
    source = source.reshape(-1, source.shape[-1])
    source = pltpu.with_memory_space_constraint(source, pltpu.HBM)
    codes = lax.all_gather(encode(target_emb.T), "src", axis=0, tiled=True)
    target = decode(codes)
    scores, row_level, col_level = find_scores(source, target, src_group, tgt_group)
    col_levels = lax.all_to_all(jnp.broadcast_to(col_level[None], (z_size,) + col_level.shape), "src", 0, 0)
    row_levels = lax.all_to_all(jnp.broadcast_to(row_level[None], (t_size,) + row_level.shape), "tgt", 0, 0)
    return find_margins(scores, row_levels, col_levels)


def solution(mesh):
    in_specs = (P("src", "tgt"), P("tgt", "src"), P("src"), P("tgt"))
    out_specs = P("src", "tgt")
    return jax.shard_map(local, mesh=mesh, in_specs=in_specs, out_specs=out_specs, check_vma=False)
```

```python
import math

import jax
import jax.numpy as jnp
from jax import lax
from jax.experimental import pallas as pl
from jax.experimental.pallas import tpu as pltpu
from jax.sharding import PartitionSpec as P

smoothing_divisor = 256.0
floor_value = -1e30
absent_below = -1e29
eps = 1e-06
lanes = 128
code_scale = 512.0
near_range = 100.0
log2_e = math.log2(math.e)


def encode(x):
    wide = x.astype(jnp.float32)
    root = jnp.sqrt(jnp.abs(wide)) * code_scale
    return jnp.where(wide < 0, -root, root).astype(jnp.float16)


def decode(code):
    wide = code.astype(jnp.float32)
    return (wide * jnp.abs(wide) * (1.0 / code_scale**2)).astype(jnp.bfloat16)


def log_sum(levels):
    highest = jnp.max(levels, axis=0)
    return highest + jnp.log2(jnp.sum(jnp.exp2(levels - highest[None]), axis=0))


def as_column(line):
    return jnp.transpose(jnp.broadcast_to(line, (lanes, lanes)))


def as_line(column):
    return jnp.transpose(jnp.broadcast_to(column, (lanes, lanes)))[:1]


def joined(lines):
    return jnp.concatenate([lines[i : i + 1, :] for i in range(lines.shape[0])], axis=1)


def level(highest, total):
    return jnp.where(highest < absent_below, floor_value, highest + jnp.log2(total))


def inverse_norm(features):
    depth, count = features.shape
    squares = jnp.zeros((8, count), jnp.float32)
    step = 64
    for k in range(0, depth, step):
        wide = features[k : k + step, :].astype(jnp.float32)
        squares += jnp.sum((wide * wide).reshape(step // 8, 8, count), axis=0)
    return lax.rsqrt(jnp.sum(squares, axis=0, keepdims=True) + eps)


def score_kernel(
    source_far, target, source_group, target_group, scores, row_out, col_out, source, turned, scale_cols, group_cols, sems
):
    depth, rows = source.shape
    columns = target.shape[1]
    size = depth // sems.shape[0]
    fetches = []
    for k in range(sems.shape[0]):
        block = slice(k * size, (k + 1) * size)
        fetches.append(pltpu.make_async_copy(source_far.at[block, :], source.at[block, :], sems.at[k]))
        fetches[-1].start()
    target_scale = inverse_norm(target)
    for i in range(rows // lanes):
        group_cols[i * lanes : (i + 1) * lanes, :] = as_column(source_group[i : i + 1, :])
    for k, fetch in enumerate(fetches):
        fetch.wait()
        block = slice(k * size, (k + 1) * size)
        for i in range(rows // lanes):
            span = slice(i * lanes, (i + 1) * lanes)
            turned[span, block] = jnp.transpose(source[block, span])
    source_scale = inverse_norm(source) * (smoothing_divisor * log2_e)
    for i in range(rows // lanes):
        span = slice(i * lanes, (i + 1) * lanes)
        scale_cols[span, :] = as_column(source_scale[:, span])

    products = jnp.dot(turned[...], target[...], preferred_element_type=jnp.float32)
    scaled = products * scale_cols[:, :1] * target_scale
    allowed = group_cols[:, :1] == joined(target_group)
    scores[...] = jnp.where(allowed, scaled, floor_value)

    col_max = jnp.max(scores[...], axis=0, keepdims=True)
    col_sum = jnp.zeros((1, columns), jnp.float32)
    row_lines = []
    for i in range(rows // lanes):
        part = scores[i * lanes : (i + 1) * lanes, :]
        row_max = jnp.max(part, axis=1, keepdims=True)
        row_sum = jnp.sum(jnp.exp2(part - row_max), axis=1, keepdims=True)
        row_lines.append(as_line(level(row_max, row_sum)))
        col_sum += jnp.sum(jnp.exp2(part - col_max), axis=0, keepdims=True)
    row_out[...] = jnp.concatenate(row_lines, axis=0)
    col_level = level(col_max, col_sum)
    col_out[...] = jnp.concatenate(
        [col_level[:, i * lanes : (i + 1) * lanes] for i in range(columns // lanes)], axis=0
    )


def margin_kernel(scores, row_levels, col_levels, margins, ready, sems):
    rows = log_sum(row_levels[...])
    cols = log_sum(col_levels[...])
    highest = jnp.maximum(jnp.max(rows), jnp.max(cols))
    lowest = jnp.minimum(jnp.min(rows), jnp.min(cols))
    near = highest - lowest < near_range

    def write(row_terms, col_term, pair_of):
        copies = []
        for i in range(rows.shape[0]):
            block = slice(i * lanes, (i + 1) * lanes)
            part = scores[block, :]
            pair = pair_of(as_column(row_terms[i : i + 1, :])[:, :1], col_term)
            ready[block, :] = jnp.where(part < absent_below, 0.0, (part - pair) * (1.0 / log2_e))
            copies.append(pltpu.make_async_copy(ready.at[block, :], margins.at[block, :], sems.at[i]))
            copies[-1].start()
        for copy in copies:
            copy.wait()

    @pl.when(near)
    def _():
        middle = highest - 1.0
        write(
            jnp.exp2(rows - highest),
            joined(jnp.exp2(cols - highest)),
            lambda row, col: jnp.log2(row + col) + middle,
        )

    @pl.when(jnp.logical_not(near))
    def _():
        write(
            rows - 1.0,
            joined(cols - 1.0),
            lambda row, col: jnp.maximum(row, col) + jnp.log2(1.0 + jnp.exp2(-jnp.abs(row - col))),
        )


def spread_kernel(part, copies, sem):
    for k in range(copies.shape[0]):
        pltpu.make_async_copy(part, copies.at[k], sem).start()
    for k in range(copies.shape[0]):
        pltpu.make_async_copy(part, copies.at[k], sem).wait()


def spread(part, count):
    return pl.pallas_call(
        spread_kernel,
        out_shape=jax.ShapeDtypeStruct((count,) + part.shape, part.dtype),
        in_specs=[pl.BlockSpec(memory_space=pltpu.VMEM)],
        out_specs=pl.BlockSpec(memory_space=pltpu.HBM),
        scratch_shapes=[pltpu.SemaphoreType.DMA],
        name="spread",
    )(part)


def find_scores(source, target, src_group, tgt_group):
    rows, columns = source.shape[1], target.shape[1]
    vmem = pl.BlockSpec(memory_space=pltpu.VMEM)
    return pl.pallas_call(
        score_kernel,
        out_shape=(
            jax.ShapeDtypeStruct((rows, columns), jnp.float32),
            jax.ShapeDtypeStruct((rows // lanes, lanes), jnp.float32),
            jax.ShapeDtypeStruct((columns // lanes, lanes), jnp.float32),
        ),
        in_specs=[pl.BlockSpec(memory_space=pltpu.HBM), vmem, vmem, vmem],
        out_specs=(vmem, vmem, vmem),
        scratch_shapes=[
            pltpu.VMEM(source.shape, jnp.bfloat16),
            pltpu.VMEM((rows, source.shape[0]), jnp.bfloat16),
            pltpu.VMEM((rows, lanes), jnp.float32),
            pltpu.VMEM((rows, lanes), jnp.int32),
            pltpu.SemaphoreType.DMA((4,)),
        ],
        compiler_params=pltpu.CompilerParams(vmem_limit_bytes=20 * 2**20),
        name="scores",
    )(source, target, src_group.reshape(-1, lanes), tgt_group.reshape(-1, lanes))


def find_margins(scores, row_levels, col_levels):
    rows, columns = scores.shape
    vmem = pl.BlockSpec(memory_space=pltpu.VMEM)
    return pl.pallas_call(
        margin_kernel,
        out_shape=jax.ShapeDtypeStruct((rows, columns), jnp.float32),
        in_specs=[vmem, vmem, vmem],
        out_specs=pl.BlockSpec(memory_space=pl.ANY),
        scratch_shapes=[
            pltpu.VMEM((rows, columns), jnp.float32),
            pltpu.SemaphoreType.DMA((rows // lanes,)),
        ],
        compiler_params=pltpu.CompilerParams(vmem_limit_bytes=16 * 2**20),
        name="margins",
    )(scores, row_levels, col_levels)


def local(source_emb, target_emb, src_group, tgt_group):
    z_size = lax.axis_size("src")
    t_size = lax.axis_size("tgt")
    source = lax.all_to_all(spread(source_emb.T, t_size), "tgt", 0, 0)
    source = source.reshape(-1, source.shape[-1])
    source = pltpu.with_memory_space_constraint(source, pltpu.HBM)
    codes = lax.all_gather(encode(target_emb.T), "src", axis=0, tiled=True)
    target = decode(codes)
    scores, row_level, col_level = find_scores(source, target, src_group, tgt_group)
    col_levels = lax.all_to_all(jnp.broadcast_to(col_level[None], (z_size,) + col_level.shape), "src", 0, 0)
    row_levels = lax.all_to_all(jnp.broadcast_to(row_level[None], (t_size,) + row_level.shape), "tgt", 0, 0)
    return find_margins(scores, row_levels, col_levels)


def solution(mesh):
    in_specs = (P("src", "tgt"), P("tgt", "src"), P("src"), P("tgt"))
    out_specs = P("src", "tgt")
    return jax.shard_map(local, mesh=mesh, in_specs=in_specs, out_specs=out_specs, check_vma=False)
```

```python
import math

import jax
import jax.numpy as jnp
from jax import lax
from jax.experimental import pallas as pl
from jax.experimental.pallas import tpu as pltpu
from jax.sharding import PartitionSpec as P

smoothing_divisor = 256.0
floor_value = -1e30
absent_below = -1e29
eps = 1e-06
lanes = 128
code_scale = 512.0
near_range = 100.0
log2_e = math.log2(math.e)


def encode(x):
    wide = x.astype(jnp.float32)
    root = jnp.sqrt(jnp.abs(wide)) * code_scale
    return jnp.where(wide < 0, -root, root).astype(jnp.float16)


def decode(code):
    wide = code.astype(jnp.float32)
    return (wide * jnp.abs(wide) * (1.0 / code_scale**2)).astype(jnp.bfloat16)


def log_sum(levels):
    highest = jnp.max(levels, axis=0)
    return highest + jnp.log2(jnp.sum(jnp.exp2(levels - highest[None]), axis=0))


def as_column(line):
    return jnp.transpose(jnp.broadcast_to(line, (lanes, lanes)))


def as_line(column):
    return jnp.transpose(jnp.broadcast_to(column, (lanes, lanes)))[:1]


def joined(lines):
    return jnp.concatenate([lines[i : i + 1, :] for i in range(lines.shape[0])], axis=1)


def level(highest, total):
    return jnp.where(highest < absent_below, floor_value, highest + jnp.log2(total))


def inverse_norm(features):
    depth, count = features.shape
    squares = jnp.zeros((8, count), jnp.float32)
    step = 64
    for k in range(0, depth, step):
        wide = features[k : k + step, :].astype(jnp.float32)
        squares += jnp.sum((wide * wide).reshape(step // 8, 8, count), axis=0)
    return lax.rsqrt(jnp.sum(squares, axis=0, keepdims=True) + eps)


def score_kernel(
    source_far, target, source_group, target_group, scores, row_out, col_out, source, turned, scale_cols, group_cols, sems
):
    depth, rows = source.shape
    columns = target.shape[1]
    size = depth // sems.shape[0]
    fetches = []
    for k in range(sems.shape[0]):
        block = slice(k * size, (k + 1) * size)
        fetches.append(pltpu.make_async_copy(source_far.at[block, :], source.at[block, :], sems.at[k]))
        fetches[-1].start()
    target_scale = inverse_norm(target)
    for i in range(rows // lanes):
        group_cols[i * lanes : (i + 1) * lanes, :] = as_column(source_group[i : i + 1, :])
    for k, fetch in enumerate(fetches):
        fetch.wait()
        block = slice(k * size, (k + 1) * size)
        for i in range(rows // lanes):
            span = slice(i * lanes, (i + 1) * lanes)
            turned[span, block] = jnp.transpose(source[block, span])
    source_scale = inverse_norm(source) * (smoothing_divisor * log2_e)
    for i in range(rows // lanes):
        span = slice(i * lanes, (i + 1) * lanes)
        scale_cols[span, :] = as_column(source_scale[:, span])

    products = jnp.dot(turned[...], target[...], preferred_element_type=jnp.float32)
    scaled = products * scale_cols[:, :1] * target_scale
    allowed = group_cols[:, :1] == joined(target_group)
    scores[...] = jnp.where(allowed, scaled, floor_value)

    col_max = jnp.max(scores[...], axis=0, keepdims=True)
    col_sum = jnp.zeros((1, columns), jnp.float32)
    row_lines = []
    for i in range(rows // lanes):
        part = scores[i * lanes : (i + 1) * lanes, :]
        row_max = jnp.max(part, axis=1, keepdims=True)
        row_sum = jnp.sum(jnp.exp2(part - row_max), axis=1, keepdims=True)
        row_lines.append(as_line(level(row_max, row_sum)))
        col_sum += jnp.sum(jnp.exp2(part - col_max), axis=0, keepdims=True)
    row_out[...] = jnp.concatenate(row_lines, axis=0)
    col_level = level(col_max, col_sum)
    col_out[...] = jnp.concatenate(
        [col_level[:, i * lanes : (i + 1) * lanes] for i in range(columns // lanes)], axis=0
    )


def margin_kernel(scores, row_levels, col_levels, margins, ready, sems):
    rows = log_sum(row_levels[...])
    cols = log_sum(col_levels[...])
    highest = jnp.maximum(jnp.max(rows), jnp.max(cols))
    lowest = jnp.minimum(jnp.min(rows), jnp.min(cols))
    near = highest - lowest < near_range

    def write(row_terms, col_term, pair_of):
        copies = []
        size = scores.shape[0] // sems.shape[0]
        for k in range(sems.shape[0]):
            block = slice(k * size, (k + 1) * size)
            i, first = divmod(k * size, lanes)
            part = scores[block, :]
            pair = pair_of(as_column(row_terms[i : i + 1, :])[first : first + size, :1], col_term)
            ready[block, :] = jnp.where(part < absent_below, 0.0, (part - pair) * (1.0 / log2_e))
            copies.append(pltpu.make_async_copy(ready.at[block, :], margins.at[block, :], sems.at[k]))
            copies[-1].start()
        for copy in copies:
            copy.wait()

    @pl.when(near)
    def _():
        middle = highest - 1.0
        write(
            jnp.exp2(rows - highest),
            joined(jnp.exp2(cols - highest)),
            lambda row, col: jnp.log2(row + col) + middle,
        )

    @pl.when(jnp.logical_not(near))
    def _():
        write(
            rows - 1.0,
            joined(cols - 1.0),
            lambda row, col: jnp.maximum(row, col) + jnp.log2(1.0 + jnp.exp2(-jnp.abs(row - col))),
        )


def spread_kernel(part, copies, sem):
    for k in range(copies.shape[0]):
        pltpu.make_async_copy(part, copies.at[k], sem).start()
    for k in range(copies.shape[0]):
        pltpu.make_async_copy(part, copies.at[k], sem).wait()


def spread(part, count):
    return pl.pallas_call(
        spread_kernel,
        out_shape=jax.ShapeDtypeStruct((count,) + part.shape, part.dtype),
        in_specs=[pl.BlockSpec(memory_space=pltpu.VMEM)],
        out_specs=pl.BlockSpec(memory_space=pltpu.HBM),
        scratch_shapes=[pltpu.SemaphoreType.DMA],
        name="spread",
    )(part)


def find_scores(source, target, src_group, tgt_group):
    rows, columns = source.shape[1], target.shape[1]
    vmem = pl.BlockSpec(memory_space=pltpu.VMEM)
    return pl.pallas_call(
        score_kernel,
        out_shape=(
            jax.ShapeDtypeStruct((rows, columns), jnp.float32),
            jax.ShapeDtypeStruct((rows // lanes, lanes), jnp.float32),
            jax.ShapeDtypeStruct((columns // lanes, lanes), jnp.float32),
        ),
        in_specs=[pl.BlockSpec(memory_space=pltpu.HBM), vmem, vmem, vmem],
        out_specs=(vmem, vmem, vmem),
        scratch_shapes=[
            pltpu.VMEM(source.shape, jnp.bfloat16),
            pltpu.VMEM((rows, source.shape[0]), jnp.bfloat16),
            pltpu.VMEM((rows, lanes), jnp.float32),
            pltpu.VMEM((rows, lanes), jnp.int32),
            pltpu.SemaphoreType.DMA((4,)),
        ],
        compiler_params=pltpu.CompilerParams(vmem_limit_bytes=20 * 2**20),
        name="scores",
    )(source, target, src_group.reshape(-1, lanes), tgt_group.reshape(-1, lanes))


def find_margins(scores, row_levels, col_levels):
    rows, columns = scores.shape
    vmem = pl.BlockSpec(memory_space=pltpu.VMEM)
    return pl.pallas_call(
        margin_kernel,
        out_shape=jax.ShapeDtypeStruct((rows, columns), jnp.float32),
        in_specs=[vmem, vmem, vmem],
        out_specs=pl.BlockSpec(memory_space=pl.ANY),
        scratch_shapes=[
            pltpu.VMEM((rows, columns), jnp.float32),
            pltpu.SemaphoreType.DMA((16,)),
        ],
        compiler_params=pltpu.CompilerParams(vmem_limit_bytes=16 * 2**20),
        name="margins",
    )(scores, row_levels, col_levels)


def local(source_emb, target_emb, src_group, tgt_group):
    z_size = lax.axis_size("src")
    t_size = lax.axis_size("tgt")
    source = lax.all_to_all(spread(source_emb.T, t_size), "tgt", 0, 0)
    source = source.reshape(-1, source.shape[-1])
    source = pltpu.with_memory_space_constraint(source, pltpu.HBM)
    codes = lax.all_gather(encode(target_emb.T), "src", axis=0, tiled=True)
    target = decode(codes)
    scores, row_level, col_level = find_scores(source, target, src_group, tgt_group)
    col_levels = lax.all_to_all(jnp.broadcast_to(col_level[None], (z_size,) + col_level.shape), "src", 0, 0)
    row_levels = lax.all_to_all(jnp.broadcast_to(row_level[None], (t_size,) + row_level.shape), "tgt", 0, 0)
    return find_margins(scores, row_levels, col_levels)


def solution(mesh):
    in_specs = (P("src", "tgt"), P("tgt", "src"), P("src"), P("tgt"))
    out_specs = P("src", "tgt")
    return jax.shard_map(local, mesh=mesh, in_specs=in_specs, out_specs=out_specs, check_vma=False)
```
